32 devices in a mesh: row: 16 (over z, y, x), col: 2 (over core).
Axes of the slice: x: 2, y: 2, z: 4, core: 2. Of those that a mesh axis runs over, the one named last changes fastest.
Arguments:
- density: float32 [16384, 16384], P('row', 'col'), as said below
Outputs:
- product: float32 [16384, 16384], P('row', 'col')
- occupation: float32 [1], replicated
Inputs may be any that keep to these rules, and one draw needn't show every extreme that they name: density is symmetric: density[i, j] = density[j, i].
All inputs are finite; a program needn't handle non-finite values.
Results may differ from the reference program's by a relative error of at most 0.000078.
Values sent between devices are 32-bit elements; how exact they have to be, the bound alone decides.
No kernel may reach another device: no remote copies, remote signals or barrier semaphores. Data moves between devices by JAX's collectives and lax.ppermute only.
A program may use at most 128 MiB of HBM per device.

```python
import math
import jax
import jax.numpy as jnp
from jax import lax

N = 16384
PANEL = 128
STEPS = 2


def draw_density(key, part):
    key = jax.random.fold_in(key, 7)
    key_a = jax.random.fold_in(key, 1)
    key_u = jax.random.fold_in(key, 2)
    base = jax.random.normal(key_a, (N, N), jnp.float32)
    spread = jax.random.uniform(key_u, (N,), jnp.float32, 0.0, 1.15)
    sym = (base + base.T) * 0.5
    place = jnp.arange(N, dtype=jnp.float32) / N
    scales = jnp.exp(0.5 * math.log(3.0) * place + spread)
    sigma = float(STEPS * PANEL) ** (-0.25)
    return (sigma * sym * scales[:, None] * scales[None, :]).astype(jnp.float32)


def setup_inputs(seed: int = 0) -> dict:
    seeds = jax.random.split(jax.random.key(seed), 2)
    density = draw_density(jax.random.fold_in(seeds[1], 71), 0)
    return dict(density=density)


def reference(density):
    stride = N // STEPS
    columns = jnp.concatenate([density[:, s * stride:s * stride + PANEL] for s in range(STEPS)], axis=1)
    rows_all = jnp.concatenate([density[s * stride:s * stride + PANEL, :] for s in range(STEPS)], axis=0)
    product = jnp.dot(columns, rows_all, precision=lax.Precision.HIGHEST, preferred_element_type=jnp.float32)
    trace_value = jnp.sum(jnp.diagonal(product)) / (N * math.sqrt(STEPS * PANEL))
    return (product, jnp.reshape(trace_value, (1,)).astype(jnp.float32))
```

```python
import functools
import math

import jax
import jax.numpy as jnp
from jax import lax
from jax.experimental import pallas as pl
from jax.experimental.pallas import tpu as pltpu
from jax.sharding import PartitionSpec as P

PANEL = 128
STEPS = 2
DEPTH = PANEL * STEPS
BLOCK = 512
BOTH = ("row", "col")


VMEM = pl.BlockSpec(memory_space=pltpu.VMEM)
ANY = pl.BlockSpec(memory_space=pl.ANY)
SLAB = 256


def split(x):
    hi = x.astype(jnp.bfloat16)
    lo = (x - hi.astype(jnp.float32)).astype(jnp.bfloat16)
    return hi, lo


def join(mine, other, core):
    return jnp.concatenate(
        [jnp.where(core == 0, mine, other), jnp.where(core == 0, other, mine)], axis=1
    )


def own_kernel(mine, other, left, total, top, bottom):
    x = join(mine[...], other[...], lax.axis_index("col"))
    hi, lo = split(x)
    left[:, 0:DEPTH] = hi
    left[:, DEPTH : 2 * DEPTH] = lo
    left[:, 2 * DEPTH : 3 * DEPTH] = hi
    top[...] = x[:BLOCK]
    bottom[...] = x[BLOCK:]
    total[...] = jnp.full(total.shape, jnp.sum(x * x), jnp.float32)


def like(rows, cols=DEPTH, dtype=jnp.float32):
    return jax.ShapeDtypeStruct((rows, cols), dtype)


def in_vmem(kernel, out_shape, *arrays):
    return pl.pallas_call(
        kernel,
        out_shape=out_shape,
        in_specs=[VMEM] * len(arrays),
        out_specs=(VMEM,) * len(out_shape),
        compiler_params=pltpu.CompilerParams(vmem_limit_bytes=8 * 2**20),
    )(*arrays)


def own_rows(mine, other):
    b = BLOCK
    shapes = (like(2 * b, 3 * DEPTH, jnp.bfloat16), like(8, 128), like(b), like(b))
    return in_vmem(own_kernel, shapes, mine, other)


def stack_kernel(*refs):
    out, at = refs[-1], 0
    for ref in refs[:-1]:
        out[at : at + ref.shape[0]] = ref[...]
        at += ref.shape[0]


def stack(*arrays):
    return in_vmem(stack_kernel, (like(sum(a.shape[0] for a in arrays), PANEL),), *arrays)[0]


def plane_kernel(mine, other, total_own, token, plane, total):
    del token
    core = lax.axis_index("col")
    total[...] = total_own[...]
    for i in range(plane.shape[0] // BLOCK):
        rows = pl.ds(i * BLOCK, BLOCK)
        x = join(mine[rows, :], other[rows, :], core)
        plane[rows, :] = x
        total[...] += jnp.sum(x * x)


def plane_rows(mine, other, total, token):
    return in_vmem(plane_kernel, (like(mine.shape[0]), like(8, 128)), mine, other, total, token)


def after_kernel(token, *refs):
    refs[len(refs) // 2][...] = jnp.zeros((8, 128), jnp.float32)


def after(token, *arrays):
    count = len(arrays)
    return pl.pallas_call(
        after_kernel,
        out_shape=(like(8, 128), *(like(*a.shape) for a in arrays)),
        in_specs=[VMEM] * (1 + count),
        out_specs=(VMEM,) * (1 + count),
        input_output_aliases={1 + i: 1 + i for i in range(count)},
        compiler_params=pltpu.CompilerParams(vmem_limit_bytes=2**20),
    )(token, *arrays)


def halves_kernel(token, x, y, later, x_same, y_same, x_top, y_bottom):
    later[...] = jnp.zeros_like(later)
    h = x_top.shape[0]
    x_top[...] = x[0:h]
    y_bottom[...] = y[h : 2 * h]


def halves(token, x, y):
    rows, cols = x.shape
    return pl.pallas_call(
        halves_kernel,
        out_shape=(like(8, 128), like(rows, cols), like(rows, cols)) + (like(rows // 2, cols),) * 2,
        in_specs=[VMEM] * 3,
        out_specs=(VMEM,) * 5,
        input_output_aliases={1: 1, 2: 2},
        compiler_params=pltpu.CompilerParams(vmem_limit_bytes=2**20),
    )(token, x, y)


def multiply_kernel(blocks, n_arrays, has_product, has_sum, *refs):
    left, arrays = refs[0], refs[1 : 1 + n_arrays]
    at = 1 + n_arrays + has_product
    if has_sum:
        mine, other = refs[at], refs[at + 1]
        at += 2
    product, token = refs[at], refs[at + 1]
    right, out, place, sems = refs[at + 2 :]
    row, core = lax.axis_index("row"), lax.axis_index("col")
    z, y, x = row // 4, (row // 2) % 2, row % 2
    own_half = core == half(z)

    def load(i, source):
        array, at = source
        hi, lo = split(arrays[array][at * BLOCK : (at + 1) * BLOCK, :])
        to = pl.ds(i * BLOCK, BLOCK)
        right[to, 0:DEPTH] = hi
        right[to, DEPTH : 2 * DEPTH] = hi
        right[to, 2 * DEPTH : 3 * DEPTH] = lo

    for i, (sources, odd, dx, dy, part) in enumerate(blocks):
        if len(sources) == 2:

            @pl.when(own_half)
            def _():
                load(i, sources[0])

            @pl.when(jnp.logical_not(own_half))
            def _():
                load(i, sources[1])

        else:
            load(i, sources[0])
        chunk = (((z + odd) % 2) * 2 + (y ^ dy)) * 2 + (x ^ dx)
        place[i] = (chunk * 2 + part) * BLOCK

    if has_sum:
        token[...] = mine[...] + other[...]
    else:
        token[...] = jnp.zeros_like(token)

    def store(i):
        return pltpu.make_async_copy(
            out.at[i], product.at[:, pl.ds(pl.multiple_of(place[i], BLOCK), BLOCK)], sems.at[i]
        )

    @pl.loop(0, len(blocks))
    def _(i):
        out[i] = lax.dot_general(
            left[...],
            right[pl.ds(pl.multiple_of(i * BLOCK, BLOCK), BLOCK), :],
            (((1,), (1,)), ((), ())),
            preferred_element_type=jnp.float32,
        )
        store(i).start()

    @pl.loop(0, len(blocks))
    def _(i):
        store(i).wait()


def multiply(left, blocks, product, cols, sums=None):
    arrays, listed = [], []
    for sources, *whose in blocks:
        found = []
        for array, place in sources:
            known = [i for i, a in enumerate(arrays) if a is array]
            if not known:
                arrays.append(array)
            found.append((known[0] if known else len(arrays) - 1, place))
        listed.append((found, *whose))
    rows, count = left.shape[0], len(blocks)
    operands, in_specs = [left, *arrays], [VMEM] * (1 + len(arrays))
    aliases = {}
    if product is not None:
        aliases = {len(operands): 0}
        operands.append(product)
        in_specs.append(ANY)
    if sums is not None:
        operands += sums
        in_specs += [VMEM] * 2
    return pl.pallas_call(
        functools.partial(
            multiply_kernel, listed, len(arrays), product is not None, sums is not None
        ),
        out_shape=(
            jax.ShapeDtypeStruct((rows, cols), jnp.float32),
            jax.ShapeDtypeStruct((8, 128), jnp.float32),
        ),
        in_specs=in_specs,
        out_specs=(ANY, VMEM),
        scratch_shapes=[
            pltpu.VMEM((count * BLOCK, 3 * DEPTH), jnp.bfloat16),
            pltpu.VMEM((count, rows, BLOCK), jnp.float32),
            pltpu.SMEM((count,), jnp.int32),
            pltpu.SemaphoreType.DMA((count,)),
        ],
        input_output_aliases=aliases,
        compiler_params=pltpu.CompilerParams(vmem_limit_bytes=20 * 2**20),
        cost_estimate=pl.CostEstimate(
            flops=6 * DEPTH * rows * BLOCK * count,
            bytes_accessed=4 * rows * BLOCK * count,
            transcendentals=0,
        ),
    )(*operands)


def half(z):
    return z // 2


def moves(target):
    pairs = []
    for z in range(4):
        for y in range(2):
            for x in range(2):
                for c in range(2):
                    to = target(x, y, z, c)
                    if to is not None:
                        tx, ty, tz, tc = to
                        here = ((z * 2 + y) * 2 + x) * 2 + c
                        there = (((tz % 4) * 2 + ty) * 2 + tx) * 2 + tc
                        pairs.append((here, there))
    return pairs


CORE = moves(lambda x, y, z, c: (x, y, z, 1 - c))
X = moves(lambda x, y, z, c: (1 - x, y, z, c))
Y = moves(lambda x, y, z, c: (x, 1 - y, z, c))
Z_1 = moves(lambda x, y, z, c: (x, y, z ^ 1, c))
Z_2 = moves(lambda x, y, z, c: (x, y, z ^ 2, c))
X_FAR = moves(lambda x, y, z, c: (1 - x, y, z, c) if c != half(z) else None)
Y_FAR = moves(lambda x, y, z, c: (x, 1 - y, z, c) if c != half(z) else None)
Z_NEAR = moves(lambda x, y, z, c: (x, y, z + 1 if c == 1 else z - 1, half(z)))
Z_FAR = moves(
    lambda x, y, z, c: (x, y, z + 1, c) if c == half((z - 1) % 4) else None
)


def send(a, pairs):
    return lax.ppermute(a, BOTH, pairs)


def on_16x2(density):
    rows, cols = density.shape
    n = 16 * rows
    mul = functools.partial(multiply, cols=cols)

    panel = density[:, 0:PANEL]
    sib = send(panel, CORE)
    raw_x, raw_y = send(panel, X), send(panel, Y)
    left, total, top, bottom = own_rows(panel, sib)
    odd_t, odd_b = send(top, Z_NEAR), send(bottom, Z_NEAR)

    token, raw_x, raw_y, x_top, y_bottom = halves(total, raw_x, raw_y)
    raw_xy, raw_yx = send(x_top, Y), send(y_bottom, X)
    token, odd_t = after(token, odd_t)
    odd_t_x, odd_t_y, far_t = send(odd_t, X), send(odd_t, Y), send(odd_t, Z_FAR)
    token, odd_b = after(token, odd_b)
    odd_b_y, odd_b_x, far_b = send(odd_b, Y), send(odd_b, X), send(odd_b, Z_FAR)
    token, raw_xy, raw_yx = after(token, raw_xy, raw_yx)
    plane = stack(raw_x, raw_y, raw_xy, raw_yx)
    sib_plane = send(plane, CORE)
    token, odd_t_x = after(token, odd_t_x)
    odd_xy = send(odd_t_x, Y)
    product, token = mul(
        left,
        [
            ([(odd_t, 0)], 1, 0, 0, 0),
            ([(odd_b, 0)], 1, 0, 0, 1),
            ([(odd_t_x, 0)], 1, 1, 0, 0),
            ([(odd_t_y, 0)], 1, 0, 1, 0),
        ],
        None,
        sums=(token, token),
    )
    token, far_t = after(token, far_t)
    far_t_x = send(far_t, X_FAR)
    token, far_b = after(token, far_b)
    far_b_y = send(far_b, Y_FAR)
    far_t_y, far_b_x = send(far_t, Y_FAR), send(far_b, X_FAR)
    plane, total = plane_rows(plane, sib_plane, total, token)
    total_1 = send(total, Z_1)
    token, odd_b_y = after(total, odd_b_y)
    odd_yx = send(odd_b_y, X)
    token, total, total_1 = after(token, total, total_1)
    product, total = mul(
        left,
        [
            ([(odd_b_x, 0)], 1, 1, 0, 1),
            ([(odd_b_y, 0)], 1, 0, 1, 1),
            ([(top, 0), (far_t, 0)], 0, 0, 0, 0),
            ([(bottom, 0), (far_b, 0)], 0, 0, 0, 1),
        ],
        product,
        sums=(total, total_1),
    )
    total_2 = send(total, Z_2)
    token, far_t_x = after(total, far_t_x)
    far_xy = send(far_t_x, Y_FAR)
    token, far_b_y = after(token, far_b_y)
    far_yx = send(far_b_y, X_FAR)
    token, total, total_2 = after(token, total, total_2)
    product, total = mul(
        left,
        [
            ([(plane, 0), (far_t_x, 0)], 0, 1, 0, 0),
            ([(plane, 1), (far_b_x, 0)], 0, 1, 0, 1),
            ([(plane, 2), (far_t_y, 0)], 0, 0, 1, 0),
            ([(plane, 3), (far_b_y, 0)], 0, 0, 1, 1),
        ],
        product,
        sums=(total, total_2),
    )
    occupation = total[0, 0] / (n * math.sqrt(DEPTH))
    product, token = mul(
        left,
        [([(odd_xy, 0)], 1, 1, 1, 0), ([(odd_yx, 0)], 1, 1, 1, 1)],
        product,
    )
    product, token = mul(
        left,
        [([(plane, 4), (far_xy, 0)], 0, 1, 1, 0), ([(plane, 5), (far_yx, 0)], 0, 1, 1, 1)],
        product,
    )
    return product, jnp.reshape(occupation, (1,))


def on_any(n, density):
    rows, cols = density.shape
    core = lax.axis_index("col")
    pieces = []
    for step in range(STEPS):
        start = step * (n // STEPS)
        at = start % cols
        piece = density[:, at : at + PANEL]
        pieces.append(jnp.where(core == start // cols, piece, 0.0))
    panel = lax.psum(jnp.concatenate(pieces, axis=1), "col")
    occupation = lax.psum(jnp.sum(panel * panel), "row") / (n * math.sqrt(DEPTH))
    whole = lax.all_gather(panel, "row", tiled=True)
    mine = lax.dynamic_slice_in_dim(whole, core * cols, cols, axis=0)
    product = lax.dot_general(
        panel,
        mine,
        (((1,), (1,)), ((), ())),
        precision=lax.Precision.HIGHEST,
        preferred_element_type=jnp.float32,
    )
    return product, jnp.reshape(occupation, (1,))


def solution(mesh):
    sizes = (mesh.shape["row"], mesh.shape["col"])

    def run(density):
        n = density.shape[0]
        body = functools.partial(on_any, n)
        if sizes == (16, 2) and n == 16 * 2 * BLOCK:
            body = on_16x2
        return jax.shard_map(
            body,
            mesh=mesh,
            in_specs=(P("row", "col"),),
            out_specs=(P("row", "col"), P()),
            check_vma=False,
        )(density)

    return run
```

```python
import functools
import math

import jax
import jax.numpy as jnp
from jax import lax
from jax.experimental import pallas as pl
from jax.experimental.pallas import tpu as pltpu
from jax.sharding import PartitionSpec as P

PANEL = 128
STEPS = 2
DEPTH = PANEL * STEPS
BLOCK = 512
BOTH = ("row", "col")


VMEM = pl.BlockSpec(memory_space=pltpu.VMEM)
ANY = pl.BlockSpec(memory_space=pl.ANY)
SLAB = 512
LIGHT = pl.CostEstimate(flops=1, bytes_accessed=1, transcendentals=0)
HEAVY = pl.CostEstimate(flops=10**10, bytes_accessed=10**8, transcendentals=0)


def split(x):
    hi = x.astype(jnp.bfloat16)
    lo = (x - hi.astype(jnp.float32)).astype(jnp.bfloat16)
    return hi, lo


def join(mine, other, core):
    return jnp.concatenate(
        [jnp.where(core == 0, mine, other), jnp.where(core == 0, other, mine)], axis=1
    )


def own_kernel(mine, other, left, total, top, bottom, again):
    again[...] = mine[...]
    x = join(mine[...], other[...], lax.axis_index("col"))
    hi, lo = split(x)
    left[:, 0:DEPTH] = hi
    left[:, DEPTH : 2 * DEPTH] = lo
    left[:, 2 * DEPTH : 3 * DEPTH] = hi
    top[...] = x[:BLOCK]
    bottom[...] = x[BLOCK:]
    total[...] = jnp.full(total.shape, jnp.sum(x * x), jnp.float32)


def like(rows, cols=DEPTH, dtype=jnp.float32):
    return jax.ShapeDtypeStruct((rows, cols), dtype)


def in_vmem(kernel, out_shape, *arrays):
    return pl.pallas_call(
        kernel,
        out_shape=out_shape,
        in_specs=[VMEM] * len(arrays),
        out_specs=(VMEM,) * len(out_shape),
        compiler_params=pltpu.CompilerParams(vmem_limit_bytes=8 * 2**20),
        cost_estimate=LIGHT,
    )(*arrays)


def own_rows(mine, other):
    b = BLOCK
    shapes = (like(2 * b, 3 * DEPTH, jnp.bfloat16), like(8, 128), like(b), like(b), like(2 * b, PANEL))
    return in_vmem(own_kernel, shapes, mine, other)


def stack_kernel(*refs):
    out, at = refs[-1], 0
    for ref in refs[:-1]:
        out[at : at + ref.shape[0]] = ref[...]
        at += ref.shape[0]


def stack(*arrays):
    rows, cols = sum(a.shape[0] for a in arrays), arrays[0].shape[1]
    return in_vmem(stack_kernel, (like(rows, cols),), *arrays)[0]


def plane_kernel(mine, other, total_own, token, plane, total):
    del token
    core = lax.axis_index("col")
    rows = plane.shape[0] // 3
    total[...] = total_own[...]
    for i, j in ((0, 1), (1, 0), (2, 2)):
        x = join(mine[i * rows : (i + 1) * rows], other[j * rows : (j + 1) * rows], core)
        plane[i * rows : (i + 1) * rows] = x
        total[...] += jnp.sum(x * x)


def plane_rows(mine, other, total, token):
    return in_vmem(plane_kernel, (like(mine.shape[0]), like(8, 128)), mine, other, total, token)


def choose_kernel(token, far_top, far_bottom, out):
    del token
    own_half = lax.axis_index("col") == half(lax.axis_index("row") // 4)

    @pl.when(own_half)
    def _():
        out[...] = far_bottom[...]

    @pl.when(jnp.logical_not(own_half))
    def _():
        out[...] = far_top[...]


def choose(token, far_top, far_bottom):
    return in_vmem(choose_kernel, (like(*far_top.shape),), token, far_top, far_bottom)[0]


def after_kernel(token, *refs):
    refs[len(refs) // 2][...] = jnp.zeros((8, 128), jnp.float32)


def after(token, *arrays, cost=LIGHT):
    count = len(arrays)
    return pl.pallas_call(
        after_kernel,
        out_shape=(like(8, 128), *(like(*a.shape) for a in arrays)),
        in_specs=[VMEM] * (1 + count),
        out_specs=(VMEM,) * (1 + count),
        input_output_aliases={1 + i: 1 + i for i in range(count)},
        compiler_params=pltpu.CompilerParams(vmem_limit_bytes=2**20),
        cost_estimate=cost,
    )(token, *arrays)


def multiply_kernel(blocks, n_arrays, has_product, has_sum, *refs):
    left, arrays = refs[0], refs[1 : 1 + n_arrays]
    at = 1 + n_arrays + has_product
    if has_sum:
        mine, other = refs[at], refs[at + 1]
        at += 2
    product, token = refs[at], refs[at + 1]
    right, out, place, sems = refs[at + 2 :]
    row, core = lax.axis_index("row"), lax.axis_index("col")
    z, y, x = row // 4, (row // 2) % 2, row % 2
    ways = {
        "here": (x, y),
        "x": (1 - x, y),
        "y": (x, 1 - y),
        "first": (x ^ (1 - core), y ^ core),
        "second": (x ^ core, y ^ (1 - core)),
        "both": (1 - x, 1 - y),
    }

    def load(i, source):
        array, at, odd, way, part = source
        hi, lo = split(arrays[array][at * BLOCK : (at + 1) * BLOCK, :])
        to = pl.ds(i * BLOCK, BLOCK)
        right[to, 0:DEPTH] = hi
        right[to, DEPTH : 2 * DEPTH] = hi
        right[to, 2 * DEPTH : 3 * DEPTH] = lo
        from_x, from_y = ways[way]
        chunk = (((z + odd) % 2) * 2 + from_y) * 2 + from_x
        place[i] = (chunk * 2 + part) * BLOCK

    for i, sources in enumerate(blocks):
        if len(sources) == 2:
            own_half = core == half(z)

            @pl.when(own_half)
            def _():
                load(i, sources[0])

            @pl.when(jnp.logical_not(own_half))
            def _():
                load(i, sources[1])

        else:
            load(i, sources[0])

    if has_sum:
        token[...] = mine[...] + other[...]
    else:
        token[...] = jnp.zeros_like(token)

    def store(i, slab):
        rows = pl.ds(slab * SLAB, SLAB)
        return pltpu.make_async_copy(
            out.at[i, rows],
            product.at[rows, pl.ds(pl.multiple_of(place[i], BLOCK), BLOCK)],
            sems.at[i, slab],
        )

    slabs = left.shape[0] // SLAB

    @pl.loop(0, len(blocks))
    def _(i):
        for slab in range(slabs):
            rows = pl.ds(slab * SLAB, SLAB)
            out[i, rows] = lax.dot_general(
                left[rows, :],
                right[pl.ds(pl.multiple_of(i * BLOCK, BLOCK), BLOCK), :],
                (((1,), (1,)), ((), ())),
                preferred_element_type=jnp.float32,
            )
            store(i, slab).start()

    @pl.loop(0, len(blocks))
    def _(i):
        for slab in range(slabs):
            store(i, slab).wait()


def multiply(left, blocks, product, cols, sums=None):
    arrays, listed = [], []
    for sources in blocks:
        found = []
        for array, *rest in sources:
            known = [i for i, a in enumerate(arrays) if a is array]
            if not known:
                arrays.append(array)
            found.append((known[0] if known else len(arrays) - 1, *rest))
        listed.append(found)
    rows, count = left.shape[0], len(blocks)
    operands, in_specs = [left, *arrays], [VMEM] * (1 + len(arrays))
    aliases = {}
    if product is not None:
        aliases = {len(operands): 0}
        operands.append(product)
        in_specs.append(ANY)
    if sums is not None:
        operands += sums
        in_specs += [VMEM] * 2
    return pl.pallas_call(
        functools.partial(
            multiply_kernel, listed, len(arrays), product is not None, sums is not None
        ),
        out_shape=(
            jax.ShapeDtypeStruct((rows, cols), jnp.float32),
            jax.ShapeDtypeStruct((8, 128), jnp.float32),
        ),
        in_specs=in_specs,
        out_specs=(ANY, VMEM),
        scratch_shapes=[
            pltpu.VMEM((count * BLOCK, 3 * DEPTH), jnp.bfloat16),
            pltpu.VMEM((count, rows, BLOCK), jnp.float32),
            pltpu.SMEM((count,), jnp.int32),
            pltpu.SemaphoreType.DMA((count, rows // SLAB)),
        ],
        input_output_aliases=aliases,
        compiler_params=pltpu.CompilerParams(vmem_limit_bytes=22 * 2**20),
        cost_estimate=HEAVY,
    )(*operands)


def half(z):
    return z // 2


def moves(target):
    pairs = []
    for z in range(4):
        for y in range(2):
            for x in range(2):
                for c in range(2):
                    to = target(x, y, z, c)
                    if to is not None:
                        tx, ty, tz, tc = to
                        here = ((z * 2 + y) * 2 + x) * 2 + c
                        there = (((tz % 4) * 2 + ty) * 2 + tx) * 2 + tc
                        pairs.append((here, there))
    return pairs


CORE = moves(lambda x, y, z, c: (x, y, z, 1 - c))
FIRST = moves(lambda x, y, z, c: (1 - x, y, z, c) if c == 0 else (x, 1 - y, z, c))
SECOND = moves(lambda x, y, z, c: (x, 1 - y, z, c) if c == 0 else (1 - x, y, z, c))
Z_NEAR = moves(lambda x, y, z, c: (x, y, z + 1 if c == 1 else z - 1, half(z)))
Z_FAR = moves(
    lambda x, y, z, c: (x, y, z + 1, c) if c == half((z - 1) % 4) else None
)
Z_FAR_BY = moves(
    lambda x, y, z, c: (x, y, z + 1, 1 - c) if c == half((z - 1) % 4) else None
)
FAR_FIRST = moves(
    lambda x, y, z, c: (1 - x, y, z, c) if c != half(z) else (x, 1 - y, z, c)
)
FAR_SECOND = moves(
    lambda x, y, z, c: (x, 1 - y, z, c) if c != half(z) else (1 - x, y, z, c)
)
Z_1 = moves(lambda x, y, z, c: (x, y, z ^ 1, c))
Z_2 = moves(lambda x, y, z, c: (x, y, z ^ 2, c))


def send(name, a, pairs):
    with jax.named_scope(name):
        return lax.ppermute(a, BOTH, pairs)


def on_16x2(density):
    rows, cols = density.shape
    n = 16 * rows
    mul = functools.partial(multiply, cols=cols)

    panel = density[:, 0:PANEL]
    sib = send("sib", panel, CORE)
    raw1 = send("raw1", panel, FIRST)
    left, total, top, bottom, again = own_rows(panel, sib)
    raw2 = send("raw2", again, SECOND)
    odd_t, odd_b = send("odd_t", top, Z_NEAR), send("odd_b", bottom, Z_NEAR)

    token, raw1 = after(total, raw1)
    raw3 = send("raw3", raw1, SECOND)
    token, odd_t = after(token, odd_t)
    odd_t1, odd_t2 = send("odd_t1", odd_t, FIRST), send("odd_t2", odd_t, SECOND)
    far_t = send("far_t", odd_t, Z_FAR)
    token, raw2, raw3 = after(token, raw2, raw3)
    mine = stack(raw1, raw2, raw3)
    other = send("other", mine, CORE)
    token, odd_b = after(token, odd_b)
    odd_b1, far_b = send("odd_b1", odd_b, FIRST), send("far_b", odd_b, Z_FAR_BY)
    token, odd_t1 = after(token, odd_t1, cost=HEAVY)
    odd_t3 = send("odd_t3", odd_t1, SECOND)
    product, token = mul(
        left,
        [
            [(odd_t, 0, 1, "here", 0)],
            [(odd_t1, 0, 1, "first", 0)],
            [(odd_t2, 0, 1, "second", 0)],
        ],
        None,
        sums=(token, token),
    )
    plane, total = plane_rows(mine, other, total, token)
    far = choose(total, far_t, far_b)
    far1, far2 = send("far1", far, FAR_FIRST), send("far2", far, FAR_SECOND)
    total_1 = send("total_1", total, Z_1)
    token, odd_b1 = after(total, odd_b1)
    token, odd_b = after(token, odd_b)
    odd_b2 = send("odd_b2", odd_b, SECOND)
    token, total, total_1 = after(token, total, total_1)
    product, total = mul(
        left,
        [
            [(odd_t3, 0, 1, "both", 0)],
            [(odd_b, 0, 1, "here", 1)],
            [(odd_b1, 0, 1, "first", 1)],
        ],
        product,
        sums=(total, total_1),
    )
    total_2 = send("total_2", total, Z_2)
    token, total_2 = after(total, total_2)
    token, far1 = after(token, far1)
    far3 = send("far3", far1, FAR_SECOND)
    token, odd_b1 = after(token, odd_b1)
    odd_b3 = send("odd_b3", odd_b1, SECOND)
    token, odd_b2 = after(token, odd_b2)
    token, far2 = after(token, far2)
    far_mine = stack(far, far1, far2)
    far_other = send("far_other", far_mine, CORE)
    product, total = mul(
        left,
        [
            [(top, 0, 0, "here", 0), (far_mine, 0, 0, "here", 0)],
            [(bottom, 0, 0, "here", 1), (far_other, 0, 0, "here", 1)],
            [(plane, 0, 0, "first", 0), (far_mine, 1, 0, "x", 0)],
            [(plane, 1, 0, "first", 1), (far_other, 1, 0, "y", 1)],
            [(plane, 2, 0, "second", 0), (far_mine, 2, 0, "y", 0)],
            [(plane, 3, 0, "second", 1), (far_other, 2, 0, "x", 1)],
        ],
        product,
        sums=(total, total_2),
    )
    occupation = total[0, 0] / (n * math.sqrt(DEPTH))
    token, odd_b3 = after(total, odd_b3)
    token, far3 = after(token, far3)
    far3_other = send("far3_other", far3, CORE)
    product, token = mul(
        left,
        [
            [(odd_b2, 0, 1, "second", 1)],
            [(odd_b3, 0, 1, "both", 1)],
            [(plane, 4, 0, "both", 0), (far3, 0, 0, "both", 0)],
            [(plane, 5, 0, "both", 1), (far3_other, 0, 0, "both", 1)],
        ],
        product,
    )
    return product, jnp.reshape(occupation, (1,))


def on_any(n, density):
    rows, cols = density.shape
    core = lax.axis_index("col")
    pieces = []
    for step in range(STEPS):
        start = step * (n // STEPS)
        at = start % cols
        piece = density[:, at : at + PANEL]
        pieces.append(jnp.where(core == start // cols, piece, 0.0))
    panel = lax.psum(jnp.concatenate(pieces, axis=1), "col")
    occupation = lax.psum(jnp.sum(panel * panel), "row") / (n * math.sqrt(DEPTH))
    whole = lax.all_gather(panel, "row", tiled=True)
    mine = lax.dynamic_slice_in_dim(whole, core * cols, cols, axis=0)
    product = lax.dot_general(
        panel,
        mine,
        (((1,), (1,)), ((), ())),
        precision=lax.Precision.HIGHEST,
        preferred_element_type=jnp.float32,
    )
    return product, jnp.reshape(occupation, (1,))


def solution(mesh):
    sizes = (mesh.shape["row"], mesh.shape["col"])

    def run(density):
        n = density.shape[0]
        body = functools.partial(on_any, n)
        if sizes == (16, 2) and n == 16 * 2 * BLOCK:
            body = on_16x2
        return jax.shard_map(
            body,
            mesh=mesh,
            in_specs=(P("row", "col"),),
            out_specs=(P("row", "col"), P()),
            check_vma=False,
        )(density)

    return run
```

```python
import functools
import math

import jax
import jax.numpy as jnp
from jax import lax
from jax.experimental import pallas as pl
from jax.experimental.pallas import tpu as pltpu
from jax.sharding import PartitionSpec as P

PANEL = 128
STEPS = 2
DEPTH = PANEL * STEPS
BLOCK = 512
BOTH = ("row", "col")


VMEM = pl.BlockSpec(memory_space=pltpu.VMEM)
ANY = pl.BlockSpec(memory_space=pl.ANY)
SLAB = 512
LIGHT = pl.CostEstimate(flops=1, bytes_accessed=1, transcendentals=0)
HEAVY = pl.CostEstimate(flops=10**10, bytes_accessed=10**8, transcendentals=0)


def split(x):
    hi = x.astype(jnp.bfloat16)
    lo = (x - hi.astype(jnp.float32)).astype(jnp.bfloat16)
    return hi, lo


def join(mine, other, core):
    return jnp.concatenate(
        [jnp.where(core == 0, mine, other), jnp.where(core == 0, other, mine)], axis=1
    )


def own_kernel(mine, other, left, total, top, bottom, again):
    again[...] = mine[...]
    x = join(mine[...], other[...], lax.axis_index("col"))
    hi, lo = split(x)
    left[:, 0:DEPTH] = hi
    left[:, DEPTH : 2 * DEPTH] = lo
    left[:, 2 * DEPTH : 3 * DEPTH] = hi
    top[...] = x[:BLOCK]
    bottom[...] = x[BLOCK:]
    total[...] = jnp.full(total.shape, jnp.sum(x * x), jnp.float32)


def like(rows, cols=DEPTH, dtype=jnp.float32):
    return jax.ShapeDtypeStruct((rows, cols), dtype)


def in_vmem(kernel, out_shape, *arrays):
    return pl.pallas_call(
        kernel,
        out_shape=out_shape,
        in_specs=[VMEM] * len(arrays),
        out_specs=(VMEM,) * len(out_shape),
        compiler_params=pltpu.CompilerParams(vmem_limit_bytes=8 * 2**20),
        cost_estimate=LIGHT,
    )(*arrays)


def own_rows(mine, other):
    b = BLOCK
    shapes = (like(2 * b, 3 * DEPTH, jnp.bfloat16), like(8, 128), like(b), like(b), like(2 * b, PANEL))
    return in_vmem(own_kernel, shapes, mine, other)


def stack_kernel(*refs):
    out, at = refs[-1], 0
    for ref in refs[:-1]:
        out[at : at + ref.shape[0]] = ref[...]
        at += ref.shape[0]


def stack(*arrays):
    rows, cols = sum(a.shape[0] for a in arrays), arrays[0].shape[1]
    return in_vmem(stack_kernel, (like(rows, cols),), *arrays)[0]


def plane_kernel(mine, other, total_own, token, plane, total):
    del token
    core = lax.axis_index("col")
    rows = plane.shape[0] // 3
    total[...] = total_own[...]
    for i, j in ((0, 1), (1, 0), (2, 2)):
        x = join(mine[i * rows : (i + 1) * rows], other[j * rows : (j + 1) * rows], core)
        plane[i * rows : (i + 1) * rows] = x
        total[...] += jnp.sum(x * x)


def plane_rows(mine, other, total, token):
    return in_vmem(plane_kernel, (like(mine.shape[0]), like(8, 128)), mine, other, total, token)


def choose_kernel(token, far_top, far_bottom, out):
    del token
    own_half = lax.axis_index("col") == half(lax.axis_index("row") // 4)

    @pl.when(own_half)
    def _():
        out[...] = far_bottom[...]

    @pl.when(jnp.logical_not(own_half))
    def _():
        out[...] = far_top[...]


def choose(token, far_top, far_bottom):
    return in_vmem(choose_kernel, (like(*far_top.shape),), token, far_top, far_bottom)[0]


def after_kernel(token, *refs):
    del token
    count = len(refs) // 2
    refs[count][...] = jnp.zeros((8, 128), jnp.float32)
    for before, later in zip(refs[:count], refs[count + 1 :], strict=True):
        later[...] = before[...]


def after(token, *arrays, cost=LIGHT):
    count = len(arrays)
    return pl.pallas_call(
        after_kernel,
        out_shape=(like(8, 128), *(like(*a.shape) for a in arrays)),
        in_specs=[VMEM] * (1 + count),
        out_specs=(VMEM,) * (1 + count),
        input_output_aliases={1 + i: 1 + i for i in range(count)},
        compiler_params=pltpu.CompilerParams(vmem_limit_bytes=2 * 2**20),
        cost_estimate=cost,
    )(token, *arrays)


def scaled(total, factor):
    def kernel(total_ref, out_ref):
        out_ref[0] = jnp.max(total_ref[0:1, 0:1]) * factor

    return pl.pallas_call(
        kernel,
        out_shape=jax.ShapeDtypeStruct((1,), jnp.float32),
        in_specs=[VMEM],
        out_specs=pl.BlockSpec(memory_space=pltpu.SMEM),
        compiler_params=pltpu.CompilerParams(vmem_limit_bytes=2**20),
        cost_estimate=LIGHT,
    )(total)


def multiply_kernel(blocks, n_arrays, has_product, has_sum, *refs):
    left, arrays = refs[0], refs[1 : 1 + n_arrays]
    at = 1 + n_arrays + has_product
    if has_sum:
        mine, other = refs[at], refs[at + 1]
        at += 2
    product, token = refs[at], refs[at + 1]
    right, out, place, sems = refs[at + 2 :]
    row, core = lax.axis_index("row"), lax.axis_index("col")
    z, y, x = row // 4, (row // 2) % 2, row % 2
    ways = {
        "here": (x, y),
        "x": (1 - x, y),
        "y": (x, 1 - y),
        "first": (x ^ (1 - core), y ^ core),
        "second": (x ^ core, y ^ (1 - core)),
        "both": (1 - x, 1 - y),
    }

    def load(i, source):
        array, at, odd, way, part = source
        hi, lo = split(arrays[array][at * BLOCK : (at + 1) * BLOCK, :])
        to = pl.ds(i * BLOCK, BLOCK)
        right[to, 0:DEPTH] = hi
        right[to, DEPTH : 2 * DEPTH] = hi
        right[to, 2 * DEPTH : 3 * DEPTH] = lo
        from_x, from_y = ways[way]
        chunk = (((z + odd) % 2) * 2 + from_y) * 2 + from_x
        place[i] = (chunk * 2 + part) * BLOCK

    for i, sources in enumerate(blocks):
        if len(sources) == 2:
            own_half = core == half(z)

            @pl.when(own_half)
            def _():
                load(i, sources[0])

            @pl.when(jnp.logical_not(own_half))
            def _():
                load(i, sources[1])

        else:
            load(i, sources[0])

    if has_sum:
        token[...] = mine[...] + other[...]
    else:
        token[...] = jnp.zeros_like(token)

    def store(i, slab):
        rows = pl.ds(slab * SLAB, SLAB)
        return pltpu.make_async_copy(
            out.at[i, rows],
            product.at[rows, pl.ds(pl.multiple_of(place[i], BLOCK), BLOCK)],
            sems.at[i, slab],
        )

    slabs = left.shape[0] // SLAB

    @pl.loop(0, len(blocks))
    def _(i):
        for slab in range(slabs):
            rows = pl.ds(slab * SLAB, SLAB)
            out[i, rows] = lax.dot_general(
                left[rows, :],
                right[pl.ds(pl.multiple_of(i * BLOCK, BLOCK), BLOCK), :],
                (((1,), (1,)), ((), ())),
                preferred_element_type=jnp.float32,
            )
            store(i, slab).start()

    @pl.loop(0, len(blocks))
    def _(i):
        for slab in range(slabs):
            store(i, slab).wait()


def multiply(left, blocks, product, cols, sums=None, cost=HEAVY):
    arrays, listed = [], []
    for sources in blocks:
        found = []
        for array, *rest in sources:
            known = [i for i, a in enumerate(arrays) if a is array]
            if not known:
                arrays.append(array)
            found.append((known[0] if known else len(arrays) - 1, *rest))
        listed.append(found)
    rows, count = left.shape[0], len(blocks)
    operands, in_specs = [left, *arrays], [VMEM] * (1 + len(arrays))
    aliases = {}
    if product is not None:
        aliases = {len(operands): 0}
        operands.append(product)
        in_specs.append(ANY)
    if sums is not None:
        operands += sums
        in_specs += [VMEM] * 2
    return pl.pallas_call(
        functools.partial(
            multiply_kernel, listed, len(arrays), product is not None, sums is not None
        ),
        out_shape=(
            jax.ShapeDtypeStruct((rows, cols), jnp.float32),
            jax.ShapeDtypeStruct((8, 128), jnp.float32),
        ),
        in_specs=in_specs,
        out_specs=(ANY, VMEM),
        scratch_shapes=[
            pltpu.VMEM((count * BLOCK, 3 * DEPTH), jnp.bfloat16),
            pltpu.VMEM((count, rows, BLOCK), jnp.float32),
            pltpu.SMEM((count,), jnp.int32),
            pltpu.SemaphoreType.DMA((count, rows // SLAB)),
        ],
        input_output_aliases=aliases,
        compiler_params=pltpu.CompilerParams(vmem_limit_bytes=20 * 2**20),
        cost_estimate=cost,
    )(*operands)


def half(z):
    return z // 2


def moves(target):
    pairs = []
    for z in range(4):
        for y in range(2):
            for x in range(2):
                for c in range(2):
                    to = target(x, y, z, c)
                    if to is not None:
                        tx, ty, tz, tc = to
                        here = ((z * 2 + y) * 2 + x) * 2 + c
                        there = (((tz % 4) * 2 + ty) * 2 + tx) * 2 + tc
                        pairs.append((here, there))
    return pairs


CORE = moves(lambda x, y, z, c: (x, y, z, 1 - c))
FIRST = moves(lambda x, y, z, c: (1 - x, y, z, c) if c == 0 else (x, 1 - y, z, c))
SECOND = moves(lambda x, y, z, c: (x, 1 - y, z, c) if c == 0 else (1 - x, y, z, c))
Z_NEAR = moves(lambda x, y, z, c: (x, y, z + 1 if c == 1 else z - 1, half(z)))
Z_FAR = moves(
    lambda x, y, z, c: (x, y, z + 1, c) if c == half((z - 1) % 4) else None
)
Z_FAR_BY = moves(
    lambda x, y, z, c: (x, y, z + 1, 1 - c) if c == half((z - 1) % 4) else None
)
Z_1 = moves(lambda x, y, z, c: (x, y, z ^ 1, c))
Z_2 = moves(lambda x, y, z, c: (x, y, z ^ 2, c))


def send(name, a, pairs):
    with jax.named_scope(name):
        return lax.ppermute(a, BOTH, pairs)


def on_16x2(density):
    rows, cols = density.shape
    n = 16 * rows
    mul = functools.partial(multiply, cols=cols)

    panel = density[:, 0:PANEL]
    sib = send("sib", panel, CORE)
    raw1 = send("raw1", panel, FIRST)
    left, total, top, bottom, again = own_rows(panel, sib)
    raw2 = send("raw2", again, SECOND)
    odd_t, odd_b = send("odd_t", top, Z_NEAR), send("odd_b", bottom, Z_NEAR)

    token, raw1 = after(total, raw1)
    raw3 = send("raw3", raw1, SECOND)
    token, odd_t = after(token, odd_t)
    odd_t1, odd_t2 = send("odd_t1", odd_t, FIRST), send("odd_t2", odd_t, SECOND)
    far_t = send("far_t", odd_t, Z_FAR)
    token, raw2, raw3 = after(token, raw2, raw3)
    mine = stack(raw1, raw2, raw3)
    other = send("other", mine, CORE)
    token, odd_b = after(token, odd_b)
    odd_b1, far_b = send("odd_b1", odd_b, SECOND), send("far_b", odd_b, Z_FAR_BY)
    token, odd_t1 = after(token, odd_t1, cost=HEAVY)
    odd_t3 = send("odd_t3", odd_t1, SECOND)
    product, token = mul(
        left,
        [
            [(odd_t, 0, 1, "here", 0)],
            [(odd_t1, 0, 1, "first", 0)],
            [(odd_t2, 0, 1, "second", 0)],
        ],
        None,
        sums=(token, token),
    )
    plane, total = plane_rows(mine, other, total, token)
    far = choose(total, far_t, far_b)
    far1, far2 = send("far1", far, SECOND), send("far2", far, FIRST)
    total_1 = send("total_1", total, Z_1)
    token, odd_b1 = after(total, odd_b1)
    token, odd_b = after(token, odd_b)
    odd_b2 = send("odd_b2", odd_b, FIRST)
    token, total, total_1 = after(token, total, total_1)
    token, odd_t3 = after(token, odd_t3)
    product, total = mul(
        left,
        [
            [(odd_t3, 0, 1, "both", 0)],
            [(odd_b, 0, 1, "here", 1)],
            [(odd_b1, 0, 1, "second", 1)],
        ],
        product,
        sums=(total, total_1),
    )
    total_2 = send("total_2", total, Z_2)
    far_o = send("far_o", far, CORE)
    token, far1 = after(total, far1)
    last = send("last", stack(far1, odd_b1), FIRST)
    far1_o = send("far1_o", far1, CORE)
    token, odd_b2 = after(token, odd_b2)
    token, far2 = after(token, far2)
    far2_o = send("far2_o", far2, CORE)
    product, total = mul(
        left,
        [
            [(top, 0, 0, "here", 0), (far, 0, 0, "here", 0)],
            [(bottom, 0, 0, "here", 1), (far_o, 0, 0, "here", 1)],
            [(plane, 0, 0, "first", 0), (far1, 0, 0, "second", 0)],
            [(plane, 1, 0, "first", 1), (far1_o, 0, 0, "first", 1)],
            [(plane, 2, 0, "second", 0), (far2, 0, 0, "first", 0)],
            [(plane, 3, 0, "second", 1), (far2_o, 0, 0, "second", 1)],
            [(odd_b2, 0, 1, "first", 1)],
        ],
        product,
        sums=(total, total_2),
        cost=LIGHT,
    )
    occupation = scaled(total, 1.0 / (n * math.sqrt(DEPTH)))
    token, last = after(total, last)
    last_o = send("last_o", last, CORE)
    product, token = mul(
        left,
        [
            [(last, 1, 1, "both", 1)],
            [(plane, 4, 0, "both", 0), (last, 0, 0, "both", 0)],
        ],
        product,
    )
    product, token = mul(
        left, [[(plane, 5, 0, "both", 1), (last_o, 0, 0, "both", 1)]], product
    )
    return product, occupation


def on_any(n, density):
    rows, cols = density.shape
    core = lax.axis_index("col")
    pieces = []
    for step in range(STEPS):
        start = step * (n // STEPS)
        at = start % cols
        piece = density[:, at : at + PANEL]
        pieces.append(jnp.where(core == start // cols, piece, 0.0))
    panel = lax.psum(jnp.concatenate(pieces, axis=1), "col")
    occupation = lax.psum(jnp.sum(panel * panel), "row") / (n * math.sqrt(DEPTH))
    whole = lax.all_gather(panel, "row", tiled=True)
    mine = lax.dynamic_slice_in_dim(whole, core * cols, cols, axis=0)
    product = lax.dot_general(
        panel,
        mine,
        (((1,), (1,)), ((), ())),
        precision=lax.Precision.HIGHEST,
        preferred_element_type=jnp.float32,
    )
    return product, jnp.reshape(occupation, (1,))


def solution(mesh):
    sizes = (mesh.shape["row"], mesh.shape["col"])

    def run(density):
        n = density.shape[0]
        body = functools.partial(on_any, n)
        if sizes == (16, 2) and n == 16 * 2 * BLOCK:
            body = on_16x2
        return jax.shard_map(
            body,
            mesh=mesh,
            in_specs=(P("row", "col"),),
            out_specs=(P("row", "col"), P()),
            check_vma=False,
        )(density)

    return run
```

```python
import functools
import math

import jax
import jax.numpy as jnp
from jax import lax
from jax.experimental import pallas as pl
from jax.experimental.pallas import tpu as pltpu
from jax.sharding import PartitionSpec as P

PANEL = 128
STEPS = 2
DEPTH = PANEL * STEPS
BLOCK = 512
BOTH = ("row", "col")


VMEM = pl.BlockSpec(memory_space=pltpu.VMEM)
ANY = pl.BlockSpec(memory_space=pl.ANY)
SLAB = 256
LIGHT = pl.CostEstimate(flops=1, bytes_accessed=1, transcendentals=0)
HEAVY = pl.CostEstimate(flops=10**10, bytes_accessed=10**8, transcendentals=0)


def split(x):
    hi = x.astype(jnp.bfloat16)
    lo = (x - hi.astype(jnp.float32)).astype(jnp.bfloat16)
    return hi, lo


def join(mine, other, core):
    return jnp.concatenate(
        [jnp.where(core == 0, mine, other), jnp.where(core == 0, other, mine)], axis=1
    )


def own_kernel(mine, other, left, total, top, bottom, again):
    again[...] = mine[...]
    x = join(mine[...], other[...], lax.axis_index("col"))
    hi, lo = split(x)
    left[:, 0:DEPTH] = hi
    left[:, DEPTH : 2 * DEPTH] = lo
    left[:, 2 * DEPTH : 3 * DEPTH] = hi
    top[...] = x[:BLOCK]
    bottom[...] = x[BLOCK:]
    total[...] = jnp.full(total.shape, jnp.sum(x * x), jnp.float32)


def like(rows, cols=DEPTH, dtype=jnp.float32):
    return jax.ShapeDtypeStruct((rows, cols), dtype)


def in_vmem(kernel, out_shape, *arrays):
    return pl.pallas_call(
        kernel,
        out_shape=out_shape,
        in_specs=[VMEM] * len(arrays),
        out_specs=(VMEM,) * len(out_shape),
        compiler_params=pltpu.CompilerParams(vmem_limit_bytes=8 * 2**20),
        cost_estimate=LIGHT,
    )(*arrays)


def own_rows(mine, other):
    b = BLOCK
    shapes = (like(2 * b, 3 * DEPTH, jnp.bfloat16), like(8, 128), like(b), like(b), like(2 * b, PANEL))
    return in_vmem(own_kernel, shapes, mine, other)


def stack_kernel(*refs):
    out, at = refs[-1], 0
    for ref in refs[:-1]:
        out[at : at + ref.shape[0]] = ref[...]
        at += ref.shape[0]


def stack(*arrays):
    rows, cols = sum(a.shape[0] for a in arrays), arrays[0].shape[1]
    return in_vmem(stack_kernel, (like(rows, cols),), *arrays)[0]


def plane_kernel(mine, other, total_own, token, plane, total):
    del token
    core = lax.axis_index("col")
    rows = plane.shape[0] // 3
    total[...] = total_own[...]
    for i, j in ((0, 1), (1, 0), (2, 2)):
        x = join(mine[i * rows : (i + 1) * rows], other[j * rows : (j + 1) * rows], core)
        plane[i * rows : (i + 1) * rows] = x
        total[...] += jnp.sum(x * x)


def plane_rows(mine, other, total, token):
    return in_vmem(plane_kernel, (like(mine.shape[0]), like(8, 128)), mine, other, total, token)


def choose_kernel(token, far_top, far_bottom, out):
    del token
    own_half = lax.axis_index("col") == half(lax.axis_index("row") // 4)

    @pl.when(own_half)
    def _():
        out[...] = far_bottom[...]

    @pl.when(jnp.logical_not(own_half))
    def _():
        out[...] = far_top[...]


def choose(token, far_top, far_bottom):
    return in_vmem(choose_kernel, (like(*far_top.shape),), token, far_top, far_bottom)[0]


def after_kernel(token, *refs):
    del token
    count = len(refs) // 2
    refs[count][...] = jnp.zeros((8, 128), jnp.float32)
    for before, later in zip(refs[:count], refs[count + 1 :], strict=True):
        later[...] = before[...]


def after(token, *arrays, cost=LIGHT):
    count = len(arrays)
    return pl.pallas_call(
        after_kernel,
        out_shape=(like(8, 128), *(like(*a.shape) for a in arrays)),
        in_specs=[VMEM] * (1 + count),
        out_specs=(VMEM,) * (1 + count),
        input_output_aliases={1 + i: 1 + i for i in range(count)},
        compiler_params=pltpu.CompilerParams(vmem_limit_bytes=2 * 2**20),
        cost_estimate=cost,
    )(token, *arrays)


def scaled(total, factor):
    def kernel(total_ref, out_ref):
        out_ref[0] = jnp.max(total_ref[0:1, 0:1]) * factor

    return pl.pallas_call(
        kernel,
        out_shape=jax.ShapeDtypeStruct((1,), jnp.float32),
        in_specs=[VMEM],
        out_specs=pl.BlockSpec(memory_space=pltpu.SMEM),
        compiler_params=pltpu.CompilerParams(vmem_limit_bytes=2**20),
        cost_estimate=LIGHT,
    )(total)


def multiply_kernel(blocks, n_arrays, has_product, has_sum, *refs):
    left, arrays = refs[0], refs[1 : 1 + n_arrays]
    at = 1 + n_arrays + has_product
    if has_sum:
        mine, other = refs[at], refs[at + 1]
        at += 2
    product, token = refs[at], refs[at + 1]
    right, out, place, sems = refs[at + 2 :]
    row, core = lax.axis_index("row"), lax.axis_index("col")
    z, y, x = row // 4, (row // 2) % 2, row % 2
    ways = {
        "here": (x, y),
        "x": (1 - x, y),
        "y": (x, 1 - y),
        "first": (x ^ (1 - core), y ^ core),
        "second": (x ^ core, y ^ (1 - core)),
        "both": (1 - x, 1 - y),
    }

    def load(i, source):
        array, at, odd, way, part = source
        hi, lo = split(arrays[array][at * BLOCK : (at + 1) * BLOCK, :])
        to = pl.ds(i * BLOCK, BLOCK)
        right[to, 0:DEPTH] = hi
        right[to, DEPTH : 2 * DEPTH] = hi
        right[to, 2 * DEPTH : 3 * DEPTH] = lo
        from_x, from_y = ways[way]
        chunk = (((z + odd) % 2) * 2 + from_y) * 2 + from_x
        place[i] = (chunk * 2 + part) * BLOCK

    for i, sources in enumerate(blocks):
        if len(sources) == 2:
            own_half = core == half(z)

            @pl.when(own_half)
            def _():
                load(i, sources[0])

            @pl.when(jnp.logical_not(own_half))
            def _():
                load(i, sources[1])

        else:
            load(i, sources[0])

    if has_sum:
        token[...] = mine[...] + other[...]
    else:
        token[...] = jnp.zeros_like(token)

    def store(i, slab):
        rows = pl.ds(slab * SLAB, SLAB)
        return pltpu.make_async_copy(
            out.at[i, rows],
            product.at[rows, pl.ds(pl.multiple_of(place[i], BLOCK), BLOCK)],
            sems.at[i, slab],
        )

    slabs = left.shape[0] // SLAB

    @pl.loop(0, len(blocks))
    def _(i):
        for slab in range(slabs):
            rows = pl.ds(slab * SLAB, SLAB)
            out[i, rows] = lax.dot_general(
                left[rows, :],
                right[pl.ds(pl.multiple_of(i * BLOCK, BLOCK), BLOCK), :],
                (((1,), (1,)), ((), ())),
                preferred_element_type=jnp.float32,
            )
            store(i, slab).start()

    @pl.loop(0, len(blocks))
    def _(i):
        for slab in range(slabs):
            store(i, slab).wait()


def multiply(left, blocks, product, cols, sums=None, cost=HEAVY):
    arrays, listed = [], []
    for sources in blocks:
        found = []
        for array, *rest in sources:
            known = [i for i, a in enumerate(arrays) if a is array]
            if not known:
                arrays.append(array)
            found.append((known[0] if known else len(arrays) - 1, *rest))
        listed.append(found)
    rows, count = left.shape[0], len(blocks)
    operands, in_specs = [left, *arrays], [VMEM] * (1 + len(arrays))
    aliases = {}
    if product is not None:
        aliases = {len(operands): 0}
        operands.append(product)
        in_specs.append(ANY)
    if sums is not None:
        operands += sums
        in_specs += [VMEM] * 2
    return pl.pallas_call(
        functools.partial(
            multiply_kernel, listed, len(arrays), product is not None, sums is not None
        ),
        out_shape=(
            jax.ShapeDtypeStruct((rows, cols), jnp.float32),
            jax.ShapeDtypeStruct((8, 128), jnp.float32),
        ),
        in_specs=in_specs,
        out_specs=(ANY, VMEM),
        scratch_shapes=[
            pltpu.VMEM((count * BLOCK, 3 * DEPTH), jnp.bfloat16),
            pltpu.VMEM((count, rows, BLOCK), jnp.float32),
            pltpu.SMEM((count,), jnp.int32),
            pltpu.SemaphoreType.DMA((count, rows // SLAB)),
        ],
        input_output_aliases=aliases,
        compiler_params=pltpu.CompilerParams(vmem_limit_bytes=20 * 2**20),
        cost_estimate=cost,
    )(*operands)


def half(z):
    return z // 2


def moves(target):
    pairs = []
    for z in range(4):
        for y in range(2):
            for x in range(2):
                for c in range(2):
                    to = target(x, y, z, c)
                    if to is not None:
                        tx, ty, tz, tc = to
                        here = ((z * 2 + y) * 2 + x) * 2 + c
                        there = (((tz % 4) * 2 + ty) * 2 + tx) * 2 + tc
                        pairs.append((here, there))
    return pairs


CORE = moves(lambda x, y, z, c: (x, y, z, 1 - c))
FIRST = moves(lambda x, y, z, c: (1 - x, y, z, c) if c == 0 else (x, 1 - y, z, c))
SECOND = moves(lambda x, y, z, c: (x, 1 - y, z, c) if c == 0 else (1 - x, y, z, c))
Z_NEAR = moves(lambda x, y, z, c: (x, y, z + 1 if c == 1 else z - 1, half(z)))
Z_FAR = moves(
    lambda x, y, z, c: (x, y, z + 1, c) if c == half((z - 1) % 4) else None
)
Z_FAR_BY = moves(
    lambda x, y, z, c: (x, y, z + 1, 1 - c) if c == half((z - 1) % 4) else None
)
Z_1 = moves(lambda x, y, z, c: (x, y, z ^ 1, c))
Z_2 = moves(lambda x, y, z, c: (x, y, z ^ 2, c))


def send(name, a, pairs):
    with jax.named_scope(name):
        return lax.ppermute(a, BOTH, pairs)


def on_16x2(density):
    rows, cols = density.shape
    n = 16 * rows
    mul = functools.partial(multiply, cols=cols)

    panel = density[:, 0:PANEL]
    sib = send("sib", panel, CORE)
    raw1 = send("raw1", panel, FIRST)
    left, total, top, bottom, again = own_rows(panel, sib)
    raw2 = send("raw2", again, SECOND)
    odd_t, odd_b = send("odd_t", top, Z_NEAR), send("odd_b", bottom, Z_NEAR)

    token, raw1 = after(total, raw1)
    raw3 = send("raw3", raw1, SECOND)
    token, odd_t = after(token, odd_t)
    odd_t1, odd_t2 = send("odd_t1", odd_t, FIRST), send("odd_t2", odd_t, SECOND)
    far_t = send("far_t", odd_t, Z_FAR)
    token, raw2, raw3 = after(token, raw2, raw3)
    mine = stack(raw1, raw2, raw3)
    other = send("other", mine, CORE)
    token, odd_b = after(token, odd_b)
    odd_b1, far_b = send("odd_b1", odd_b, SECOND), send("far_b", odd_b, Z_FAR_BY)
    token, odd_t1 = after(token, odd_t1, cost=HEAVY)
    odd_t3 = send("odd_t3", odd_t1, SECOND)
    product, token = mul(
        left,
        [
            [(odd_t, 0, 1, "here", 0)],
            [(odd_t1, 0, 1, "first", 0)],
            [(odd_t2, 0, 1, "second", 0)],
        ],
        None,
        sums=(token, token),
    )
    plane, total = plane_rows(mine, other, total, token)
    far = choose(total, far_t, far_b)
    far1, far2 = send("far1", far, SECOND), send("far2", far, FIRST)
    total_1 = send("total_1", total, Z_1)
    token, odd_b1 = after(total, odd_b1)
    token, odd_b = after(token, odd_b)
    odd_b2 = send("odd_b2", odd_b, FIRST)
    token, total, total_1 = after(token, total, total_1)
    token, odd_t3 = after(token, odd_t3)
    product, total = mul(
        left,
        [
            [(odd_t3, 0, 1, "both", 0)],
            [(odd_b, 0, 1, "here", 1)],
            [(odd_b1, 0, 1, "second", 1)],
        ],
        product,
        sums=(total, total_1),
    )
    total_2 = send("total_2", total, Z_2)
    far_o = send("far_o", far, CORE)
    token, far1 = after(total, far1)
    last = send("last", stack(far1, odd_b1), FIRST)
    far1_o = send("far1_o", far1, CORE)
    token, odd_b2 = after(token, odd_b2)
    token, far2 = after(token, far2)
    far2_o = send("far2_o", far2, CORE)
    product, total = mul(
        left,
        [
            [(top, 0, 0, "here", 0), (far, 0, 0, "here", 0)],
            [(bottom, 0, 0, "here", 1), (far_o, 0, 0, "here", 1)],
            [(plane, 0, 0, "first", 0), (far1, 0, 0, "second", 0)],
            [(plane, 1, 0, "first", 1), (far1_o, 0, 0, "first", 1)],
            [(plane, 2, 0, "second", 0), (far2, 0, 0, "first", 0)],
            [(plane, 3, 0, "second", 1), (far2_o, 0, 0, "second", 1)],
            [(odd_b2, 0, 1, "first", 1)],
        ],
        product,
        sums=(total, total_2),
        cost=LIGHT,
    )
    occupation = scaled(total, 1.0 / (n * math.sqrt(DEPTH)))
    token, last = after(total, last)
    last_o = send("last_o", last, CORE)
    product, token = mul(
        left,
        [
            [(last, 1, 1, "both", 1)],
            [(plane, 4, 0, "both", 0), (last, 0, 0, "both", 0)],
        ],
        product,
    )
    product, token = mul(
        left, [[(plane, 5, 0, "both", 1), (last_o, 0, 0, "both", 1)]], product
    )
    return product, occupation


def on_any(n, density):
    rows, cols = density.shape
    core = lax.axis_index("col")
    pieces = []
    for step in range(STEPS):
        start = step * (n // STEPS)
        at = start % cols
        piece = density[:, at : at + PANEL]
        pieces.append(jnp.where(core == start // cols, piece, 0.0))
    panel = lax.psum(jnp.concatenate(pieces, axis=1), "col")
    occupation = lax.psum(jnp.sum(panel * panel), "row") / (n * math.sqrt(DEPTH))
    whole = lax.all_gather(panel, "row", tiled=True)
    mine = lax.dynamic_slice_in_dim(whole, core * cols, cols, axis=0)
    product = lax.dot_general(
        panel,
        mine,
        (((1,), (1,)), ((), ())),
        precision=lax.Precision.HIGHEST,
        preferred_element_type=jnp.float32,
    )
    return product, jnp.reshape(occupation, (1,))


def solution(mesh):
    sizes = (mesh.shape["row"], mesh.shape["col"])

    def run(density):
        n = density.shape[0]
        body = functools.partial(on_any, n)
        if sizes == (16, 2) and n == 16 * 2 * BLOCK:
            body = on_16x2
        return jax.shard_map(
            body,
            mesh=mesh,
            in_specs=(P("row", "col"),),
            out_specs=(P("row", "col"), P()),
            check_vma=False,
        )(density)

    return run
```
